32 devices in a mesh: gx: 8 (over z, core), gy: 4 (over y, x).
Axes of the slice: x: 2, y: 2, z: 4, core: 2. Of those that a mesh axis runs over, the one named last changes fastest.
Arguments:
- wavefunctions: float32 [96, 18432], P('gx', 'gy'), may hold values from -6 to 6
- potential: float32 [96, 288], P('gx', 'gy'), may hold values from -1 to 1
- cell_matrix: float32 [343, 343], replicated, may hold values from -0.08639188 to 1.4863919, as said below
- pair_cell: int32 [32, 64], P(('gx', 'gy')), may hold values from 0 to 3, as said below
- pair_tile: float32 [32, 64, 18, 343], P(('gx', 'gy')), may hold values from -0.2159797 to 0.2159797, as said below
- slot_atom: int32 [32, 64], P(('gx', 'gy')), may hold values from 0 to 63, as said below
- coupling: float32 [2048, 18, 18], P(('gx', 'gy')), may hold values from -0.28 to 0.28, as said below
- bounds: float32 [2, 3], replicated, may hold values from -2.5 to 15, as said below
Outputs:
- filtered: float32 [96, 18432], P('gx', 'gy')
The draws below stay inside these ranges and needn't reach their ends.
Inputs may be any that keep to these rules, and one draw needn't show every extreme that they name: `pair_cell`: slots d * 2 to d * 2 + 1 of a device go to owner d; each slot is live or padded, and a padded slot has cell 0. Some owner receives 2 live slots from every device in every draw. `slot_atom`: entry [d, s * 2 + k] names the atom on owner d of slot d * 2 + k of device s; padded slots name 0. `pair_tile`: padded slots hold all-zero tiles. `coupling`: each matrix is symmetric. `cell_matrix`: Symmetric. `bounds`: each row rises: lowest estimate, then lower end, then upper end.
All inputs are finite; a program needn't handle non-finite values.
Results may differ from the reference program's by a relative error of at most 0.0001.
Values sent between devices are 32-bit elements; how exact they have to be, the bound alone decides.
A program may use at most 128 MiB of HBM per device.

```python
import jax
import jax.numpy as jnp
from jax import lax

DEG = 6
NPC = 343
W = 64
NPROJ = 18
CX = 2
CY = 1
CZ = 2
ATOM_DEV = 64
CAP = 2
ORDER = 2
FILTERS = 2
OWNERS = 32
SLOTS = 64
ZN = 12
NXN = 96
NYN = 24
N_GX = 8
N_GY = 4


def live_slots(key):
    base = jax.random.fold_in(key, 7)
    key_counts, key_busy, key_full = jax.random.split(base, 3)
    counts = jax.random.randint(key_counts, (OWNERS, OWNERS), 0, CAP + 1)
    busy_owner = (jax.random.randint(key_busy, (1, OWNERS), 0, 4) == 0).astype(jnp.int32)
    counts = jnp.minimum(counts + busy_owner, CAP)
    full_owner = jax.random.randint(key_full, (), 0, OWNERS)
    counts = jnp.where(jnp.arange(OWNERS)[None, :] == full_owner, CAP, counts)
    return jnp.arange(CAP)[None, None, :] < counts[:, :, None]


def rough_values(key, shape):
    return jnp.clip(jax.random.normal(key, shape, jnp.float32), -4.0, 4.0)


def draw_pair_cell(key, part):
    live = live_slots(key).reshape(OWNERS, SLOTS)
    cell_ids = jax.random.randint(jax.random.fold_in(key, 17), (OWNERS, SLOTS), 0, CX * CY * CZ)
    return jnp.where(live, cell_ids, 0).astype(jnp.int32)


def draw_slot_atom(key, part):
    live = live_slots(key).transpose(1, 0, 2).reshape(OWNERS, SLOTS)
    atom_ids = jax.random.randint(jax.random.fold_in(key, 27), (OWNERS, SLOTS), 0, ATOM_DEV)
    return jnp.where(live, atom_ids, 0).astype(jnp.int32)


def draw_pair_tile(key, part):
    live = live_slots(key).reshape(OWNERS, SLOTS, 1, 1).astype(jnp.float32)
    values = rough_values(jax.random.fold_in(key, 37), (OWNERS, SLOTS, NPROJ, NPC))
    return values * live * (1.0 / NPC ** 0.5)


def draw_coupling(key, part):
    values = rough_values(jax.random.fold_in(key, 47), (OWNERS * ATOM_DEV, NPROJ, NPROJ))
    return (values + jnp.swapaxes(values, 1, 2)) * 0.035


def draw_cell_matrix(key, part):
    values = rough_values(jax.random.fold_in(key, 57), (NPC, NPC))
    diagonal = jax.random.uniform(jax.random.fold_in(key, 67), (NPC,), jnp.float32, 0.6, 1.4)
    return (values + values.T) * (0.2 / NPC ** 0.5) + jnp.diag(diagonal)


def draw_bounds(key, part):
    lowest = jax.random.uniform(jax.random.fold_in(key, 71), (FILTERS,), jnp.float32, -2.5, -1.5)
    lower_end = jax.random.uniform(jax.random.fold_in(key, 73), (FILTERS,), jnp.float32, 1.5, 2.5)
    upper_end = jax.random.uniform(jax.random.fold_in(key, 79), (FILTERS,), jnp.float32, 13.0, 15.0)
    return jnp.stack([lowest, lower_end, upper_end], axis=1)


def shard_levels(rng, dims, shards, least, high):
    def one(dim, shards_of):
        draws = jax.random.uniform(jax.random.fold_in(jax.random.fold_in(rng, 6), dim), (shards_of,), jnp.float32, least / len(shards), high / len(shards))
        return jnp.repeat(jnp.exp(draws), dims[dim] // shards_of).reshape((-1,) + (1,) * (len(dims) - dim - 1))

    gain = one(*shards[0])
    for cut in shards[1:]:
        gain = gain * one(*cut)
    return gain


def centred(rng, extent, scale, limit, shards=(), kind=jnp.bfloat16):
    values = scale * jax.random.normal(rng, extent, jnp.float32)
    if shards:
        values = values * shard_levels(rng, extent, shards, -0.22, 0.18)
    return jnp.clip(values, -limit, limit).astype(kind)


def setup_inputs(seed: int = 0) -> dict:
    key_list = jax.random.split(jax.random.key(seed), 9)
    return {
        "wavefunctions": centred(key_list[0], (NXN, NYN * ZN * W), 1.0, 6.0, ((0, 8), (1, 4)), jnp.float32),
        "potential": jnp.clip(jax.random.uniform(key_list[1], (NXN, NYN * ZN), jnp.float32, -1.0, 1.0) * shard_levels(key_list[1], (NXN, NYN * ZN), ((0, 8), (1, 4)), -0.4, 0.0), -1.0, 1.0),
        "cell_matrix": draw_cell_matrix(jax.random.fold_in(key_list[8], 71), 0),
        "pair_cell": draw_pair_cell(jax.random.fold_in(key_list[8], 71), 0),
        "pair_tile": draw_pair_tile(jax.random.fold_in(key_list[8], 71), 0),
        "slot_atom": draw_slot_atom(jax.random.fold_in(key_list[8], 71), 0),
        "coupling": draw_coupling(jax.random.fold_in(key_list[8], 71), 0),
        "bounds": draw_bounds(jax.random.fold_in(key_list[8], 71), 0),
    }


PRECISE = lax.Precision.HIGHEST


def split_lead(values, number):
    trailing = values.shape[1:]
    leading_part = values[: number * DEG].reshape((number, DEG) + trailing)
    upper_part = values[DEG::DEG][:, None]
    return jnp.concatenate([leading_part, upper_part], axis=1)


def join_lead(values):
    number = values.shape[0]
    trailing = values.shape[2:]
    leading_part = values[:, :DEG].reshape((number * DEG,) + trailing)
    leading_part = jnp.concatenate([leading_part, jnp.zeros((1,) + trailing, jnp.float32)], axis=0)
    upper_part = jnp.zeros((number + 1, DEG) + trailing, jnp.float32).at[1:, 0].set(values[:, DEG])
    upper_part = upper_part.reshape(((number + 1) * DEG,) + trailing)[: number * DEG + 1]
    return leading_part + upper_part


def gather_cells(extended, cells_x, cells_y, cells_z):
    closed = jnp.concatenate([extended, extended[:, :, :1]], axis=2)
    layered = split_lead(closed, cells_x)
    layered = split_lead(jnp.moveaxis(layered, 2, 0), cells_y)
    layered = split_lead(jnp.moveaxis(layered, 4, 0), cells_z)
    layered = layered.transpose(5, 3, 1, 4, 2, 0, 6)
    return layered.reshape((DEG + 1) ** 3, cells_x * cells_y * cells_z, layered.shape[-1])


def scatter_cells(cell_out, cells_x, cells_y, cells_z):
    columns = cell_out.shape[-1]
    layered = cell_out.reshape(DEG + 1, DEG + 1, DEG + 1, cells_x, cells_y, cells_z, columns)
    layered = layered.transpose(5, 2, 4, 1, 3, 0, 6)
    layered = join_lead(layered)
    layered = layered[:-1].at[0].add(layered[-1])
    layered = join_lead(jnp.moveaxis(layered, 0, 4))
    layered = join_lead(jnp.moveaxis(layered, 0, 3))
    return layered.transpose(0, 2, 1, 3)


def apply_operator(current, node_potential, cell_matrix, pair_cell, pair_tile, slot_atom, coupling):
    cells_x = NXN // DEG
    cells_y = NYN // DEG
    extended = jnp.concatenate([current, current[:1]], axis=0)
    extended = jnp.concatenate([extended, extended[:, :1]], axis=1)
    cell_in = gather_cells(extended, cells_x, cells_y, CZ)
    kinetic = jnp.dot(cell_matrix, cell_in.reshape(NPC, -1), precision=PRECISE).reshape(cell_in.shape)
    by_device = cell_in.reshape(NPC, N_GX, CX, N_GY, CY, CZ, W).transpose(1, 3, 0, 2, 4, 5, 6)
    by_device = by_device.reshape(OWNERS, NPC, CX * CY * CZ, W)

    def project(members):
        device_cells, cell_ids, tile_set = members
        picked = jnp.take(device_cells, cell_ids, axis=1)
        return jnp.einsum("spn,nsw->spw", tile_set, picked, precision=PRECISE)

    projected = lax.map(project, (by_device, pair_cell, pair_tile))
    at_owner = projected.reshape(OWNERS, OWNERS, CAP, NPROJ, W).transpose(1, 0, 2, 3, 4)
    at_owner = at_owner.reshape(OWNERS, SLOTS, NPROJ, W)
    one_hot = (slot_atom[:, :, None] == jnp.arange(ATOM_DEV, dtype=jnp.int32)[None, None, :]).astype(jnp.float32)
    atom_sums = jnp.einsum("dsa,dspw->dapw", one_hot, at_owner, precision=PRECISE)
    applied = jnp.einsum("dapq,daqw->dapw", coupling.reshape(OWNERS, ATOM_DEV, NPROJ, NPROJ), atom_sums, precision=PRECISE)
    answers = jnp.einsum("dsa,dapw->dspw", one_hot, applied, precision=PRECISE)
    returned = answers.reshape(OWNERS, OWNERS, CAP, NPROJ, W).transpose(1, 0, 2, 3, 4)
    returned = returned.reshape(OWNERS, SLOTS, NPROJ, W)

    def deposit(members):
        cell_ids, tile_set, coeffs = members
        spread = jnp.einsum("spn,spw->nsw", tile_set, coeffs, precision=PRECISE)
        return jnp.zeros((NPC, CX * CY * CZ, W), jnp.float32).at[:, cell_ids].add(spread)

    deposits = lax.map(deposit, (pair_cell, pair_tile, returned))
    projector_part = deposits.reshape(N_GX, N_GY, NPC, CX, CY, CZ, W).transpose(2, 0, 3, 1, 4, 5, 6)
    projector_part = projector_part.reshape(NPC, cells_x * cells_y * CZ, W)
    summed = scatter_cells(kinetic + projector_part, cells_x, cells_y, CZ)
    summed = summed[:, :-1].at[:, 0].add(summed[:, -1])
    summed = summed[:-1].at[0].add(summed[-1])
    return summed + node_potential * current


def reference(wavefunctions, potential, cell_matrix, pair_cell, pair_tile, slot_atom, coupling, bounds):
    node_potential = potential.reshape(NXN, NYN, ZN, 1)
    previous = wavefunctions.reshape(NXN, NYN, ZN, W)

    def operator(field):
        return apply_operator(field, node_potential, cell_matrix, pair_cell, pair_tile, slot_atom, coupling)

    for filter_index in range(FILTERS):
        lower_bound = bounds[filter_index, 0]
        low_end = bounds[filter_index, 1]
        high_end = bounds[filter_index, 2]
        half_width = (high_end - low_end) / 2.0
        centre = (high_end + low_end) / 2.0
        sigma_now = half_width / (lower_bound - centre)
        gamma_term = 2.0 / sigma_now
        current = (sigma_now / half_width) * (operator(previous) - centre * previous)
        for repeat in range(ORDER - 1):
            sigma_next = 1.0 / (gamma_term - sigma_now)
            following = (2.0 * sigma_next / half_width) * (operator(current) - centre * current) - (sigma_now * sigma_next) * previous
            previous = current
            current = following
            sigma_now = sigma_next
        previous = current
    return previous.reshape(NXN, NYN * ZN * W)
```

```python
import jax
import jax.numpy as jnp
from jax import lax
from jax.sharding import PartitionSpec as P

DEG = 6
W = 64
CX = 2
CZ = 2
FILTERS = 2
ZN = 12
NPROJ = 18
CAP = 2
PAD = 24
ZP = 8
HALF = CZ * W

FINE = lax.Precision.HIGHEST
HIGH = lax.Precision.HIGH


def shifted(value, axis, steps):
    count = lax.axis_size(axis)
    pairs = [(source, (source + steps) % count) for source in range(count)]
    return lax.ppermute(value, axis, pairs)


def to_cells(extended):
    closed = jnp.concatenate([extended, extended[:, :, :1]], axis=2)
    blocks = []
    for p in range(CX):
        for r in range(CZ):
            block = closed[p * DEG : p * DEG + DEG + 1, :, r * DEG : r * DEG + DEG + 1]
            block = jnp.pad(block, ((0, 0), (0, 0), (0, ZP - DEG - 1), (0, 0)))
            blocks.append(jnp.broadcast_to(block, block.shape[:3] + (W,)))
    return jnp.concatenate(blocks, axis=3)


def to_nodes(state):
    rows = []
    for p in range(CX):
        parts = [
            state[:DEG, :DEG, :DEG, (p * CZ + r) * W : (p * CZ + r + 1) * W] for r in range(CZ)
        ]
        rows.append(jnp.concatenate(parts, axis=2))
    return jnp.concatenate(rows, axis=0)


def swap_z(face):
    return jnp.concatenate(
        [face[..., (i ^ 1) * W : ((i ^ 1) + 1) * W] for i in range(CX * CZ)], axis=-1
    )


def sum_shared(parts):
    plane = parts[:, :, 0] + swap_z(parts[:, :, DEG])
    parts = jnp.concatenate(
        [plane[:, :, None], parts[:, :, 1:DEG], swap_z(plane)[:, :, None], parts[:, :, DEG + 1 :]],
        axis=2,
    )
    low, high = parts[0, :, :, :HALF], parts[DEG, :, :, HALF:]
    middle = parts[DEG, :, :, :HALF] + parts[0, :, :, HALF:]
    from_right = shifted(low.reshape(-1, HALF), "gx", -1).reshape(low.shape)
    from_left = shifted(high.reshape(-1, HALF), "gx", 1).reshape(low.shape)
    first = jnp.concatenate([low + from_left, middle], axis=-1)
    last = jnp.concatenate([middle, high + from_right], axis=-1)
    parts = jnp.concatenate([first[None], parts[1:DEG], last[None]], axis=0)
    low, high = parts[:, 0], parts[:, DEG]
    from_right = shifted(low.reshape(-1, 2 * HALF), "gy", -1).reshape(low.shape)
    from_left = shifted(high.reshape(-1, 2 * HALF), "gy", 1).reshape(low.shape)
    return jnp.concatenate(
        [(low + from_left)[:, None], parts[:, 1:DEG], (high + from_right)[:, None]], axis=1
    )


def body(wavefunctions, potential, cell_matrix, pair_cell, pair_tile, slot_atom, coupling, bounds):
    rows_x = wavefunctions.shape[0]
    rows_y = potential.shape[1] // ZN
    owners = pair_cell.shape[1] // CAP
    atoms = coupling.shape[0]
    side = DEG + 1
    nodes = side * side * ZP
    lanes = CX * HALF
    rows = owners * PAD

    joined = jnp.concatenate(
        [wavefunctions.reshape(rows_x, rows_y, ZN * W), potential.reshape(rows_x, rows_y, ZN)],
        axis=2,
    )
    face_in = shifted(joined[:1].reshape(1, -1), "gx", -1)
    joined = jnp.concatenate([joined, face_in.reshape((1,) + joined.shape[1:])], axis=0)
    side_in = shifted(joined[:, 0], "gy", -1)
    joined = jnp.concatenate([joined, side_in[:, None]], axis=1)
    field = joined[:, :, : ZN * W].reshape(rows_x + 1, rows_y + 1, ZN, W)
    start = to_cells(field).reshape(nodes, lanes)
    pot = to_cells(joined[:, :, ZN * W :, None]).reshape(nodes, lanes)

    def pad_nodes(values):
        lead = values.shape[:-1]
        values = values.reshape(lead + (side, side, side))
        values = jnp.pad(values, [(0, 0)] * (len(lead) + 2) + [(0, ZP - side)])
        return values.reshape(lead + (nodes,))

    kinetic = pad_nodes(pad_nodes(cell_matrix).T)
    tiles = pad_nodes(pair_tile[0].reshape(owners, CAP, NPROJ, -1).transpose(1, 0, 2, 3))
    tiles = jnp.pad(tiles, ((0, 0), (0, 0), (0, PAD - NPROJ), (0, 0))).reshape(CAP * rows, nodes)
    cells = jnp.repeat(pair_cell[0].reshape(owners, CAP).T, PAD, axis=1).reshape(CAP * rows, 1)
    masks = [(cells == c).astype(jnp.float32) for c in range(CX * CZ)]
    spread_matrix = jnp.concatenate([kinetic, tiles.T], axis=1)

    atom_index = slot_atom[0].reshape(owners, CAP)
    coupled = jnp.pad(coupling, ((0, 0), (0, PAD - NPROJ), (0, PAD - NPROJ)))
    small = (CAP * rows) ** 2 * 4 <= 16 * 2**20
    if small:
        by_slot = jnp.take(coupled, atom_index.T.reshape(-1), axis=0).reshape(CAP * rows, PAD)
        repeat = jnp.tile(jnp.eye(PAD, dtype=jnp.float32), (1, CAP * owners))
        names = jnp.repeat(atom_index.T.reshape(-1), PAD)
        routed = jnp.where(
            names[:, None] == names[None, :], jnp.dot(by_slot, repeat, precision=FINE), 0.0
        )
    else:
        one_hot = (
            atom_index[:, :, None] == jnp.arange(atoms, dtype=jnp.int32)[None, None, :]
        ).astype(jnp.float32)

    def owner_work(received):
        if small:
            stacked = jnp.concatenate([received[:, :W], received[:, W:]], axis=0)
            out = jnp.dot(routed, stacked, precision=HIGH)
            return jnp.concatenate([out[:rows], out[rows:]], axis=1)
        values = received.reshape(owners, PAD, CAP, W)
        sums = jnp.einsum("sqkw,ska->aqw", values, one_hot, precision=HIGH)
        applied = jnp.einsum("apq,aqw->apw", coupled, sums, precision=HIGH)
        back = jnp.einsum("apw,ska->spkw", applied, one_hot, precision=HIGH)
        return back.reshape(rows, CAP * W)

    def exchange(values):
        return lax.all_to_all(values, ("gx", "gy"), split_axis=0, concat_axis=0, tiled=True)

    def apply_cells(current):
        raw = jnp.dot(tiles, current, precision=HIGH)
        picked = sum(masks[c] * raw[:, c * W : (c + 1) * W] for c in range(CX * CZ))
        projected = jnp.concatenate([picked[:rows], picked[rows:]], axis=1)
        returned = exchange(owner_work(exchange(projected)))
        returned = jnp.concatenate([returned[:, :W], returned[:, W:]], axis=0)
        spread = jnp.concatenate([masks[c] * returned for c in range(CX * CZ)], axis=1)
        out = jnp.dot(spread_matrix, jnp.concatenate([current, spread], axis=0), precision=HIGH)
        return sum_shared(out.reshape(side, side, ZP, lanes)).reshape(nodes, lanes)

    previous = start
    for filter_index in range(FILTERS):
        lower_bound = bounds[filter_index, 0]
        low_end = bounds[filter_index, 1]
        high_end = bounds[filter_index, 2]
        half_width = (high_end - low_end) / 2.0
        centre = (high_end + low_end) / 2.0
        sigma_now = half_width / (lower_bound - centre)
        gamma_term = 2.0 / sigma_now
        shift = pot - centre
        current = sigma_now / half_width * (apply_cells(previous) + shift * previous)
        sigma_next = 1.0 / (gamma_term - sigma_now)
        following = (
            2.0 * sigma_next / half_width * (apply_cells(current) + shift * current)
            - sigma_now * sigma_next * previous
        )
        previous = following
    return to_nodes(previous.reshape(side, side, ZP, lanes)).reshape(rows_x, rows_y * ZN * W)


def solution(mesh):
    placed = (
        P("gx", "gy"),
        P("gx", "gy"),
        P(),
        P(("gx", "gy"), None),
        P(("gx", "gy"), None, None, None),
        P(("gx", "gy"), None),
        P(("gx", "gy"), None, None),
        P(),
    )
    return jax.shard_map(body, mesh=mesh, in_specs=placed, out_specs=P("gx", "gy"), check_vma=False)
```
